32 devices in a mesh: group: 4 (over y, core), seq: 4 (over z), mp: 2 (over x).
Axes of the slice: x: 2, y: 2, z: 4, core: 2. Of those that a mesh axis runs over, the one named last changes fastest.
Arguments:
- gen_hidden: bfloat16 [4, 64, 2048], P('seq', ('group', 'mp')), may hold values from -6 to 6
- gen_gain: float32 [2048], replicated, may hold values from 0.5 to 1.5
- head_weight: bfloat16 [2048, 64], replicated, may hold values from -0.125 to 0.125
- noise: float32 [4, 64, 64], P('seq', ('group', 'mp')), may hold values from -6 to 6
- timestep: int32 [1], replicated, may hold values from 20 to 980
- stream: bfloat16 [4, 64, 5120], P('seq', None, 'mp'), may hold values from -60 to 60
- patch_weight: bfloat16 [64, 5120], P(None, 'mp'), may hold values from -0.75 to 0.75
- conditions: float32 [4, 5120], P('group', 'mp'), may hold values from -6 to 6
- teacher_qkv: bfloat16 [5120, 3, 4, 128], P('mp', None, 'seq'), may hold values from -0.078125 to 0.078125
- teacher_out: bfloat16 [4, 128, 64], P('seq'), may hold values from -0.25 to 0.25
- fake_qkv: bfloat16 [5120, 3, 4, 128], P('mp', None, 'seq'), may hold values from -0.078125 to 0.078125
- fake_out: bfloat16 [4, 128, 64], P('seq'), may hold values from -0.25 to 0.25
Outputs:
- score_gap: float32 [4, 64, 64], P('seq', ('group', 'mp'))
- grad_hidden: bfloat16 [4, 64, 2048], P('seq', ('group', 'mp'))
The draws below stay inside these ranges and needn't reach their ends.
All inputs are finite; a program needn't handle non-finite values.
Results may differ from the reference program's by a relative error of at most 0.02.
The reference program's roundings to bfloat16 on the way count: a program that leaves them out, or rounds other values in their place, can miss the bound.
Values may be sent and summed in bfloat16 or wider, within the bound.
A program may use at most 64 MiB of HBM per device.

```python
import jax
import jax.numpy as jnp
from jax import lax

D_S = 5120
DG = 2048
LAT = 64
HEAD_DIM = 128
TOK_DEV = 64
HEADS = 4
N_GROUP = 4
N_SEQ = 4
N_MP = 2


def draw_stream(key, part):
    key = jax.random.fold_in(key, 11)
    key_base = jax.random.fold_in(key, 0)
    values = jnp.clip(jax.random.normal(key_base, (N_SEQ, TOK_DEV, D_S), jnp.float32), -6.0, 6.0)
    return values.astype(jnp.bfloat16)


def levels(key, dims, pieces, low, high):
    factor_of = 1.0
    for position, shards_of in pieces:
        draws = jax.random.uniform(jax.random.fold_in(jax.random.fold_in(key, 6), position), (shards_of,), jnp.float32, low / len(pieces), high / len(pieces))
        factor_of = factor_of * jnp.repeat(jnp.exp(draws), dims[position] // shards_of).reshape((-1,) + (1,) * (len(dims) - 1 - position))
    return factor_of


def gaussian(key, shape, scale, limit, cuts=(), dtype=jnp.bfloat16):
    drawn = scale * jax.random.normal(key, shape, jnp.float32)
    if cuts:
        drawn = drawn * levels(key, shape, cuts, -0.22, 0.18)
    return jnp.clip(drawn, -limit, limit).astype(dtype)


def setup_inputs(seed: int = 0) -> dict:
    splits = jax.random.split(jax.random.key(seed), 13)
    return {
        "gen_hidden": gaussian(splits[0], (N_SEQ, TOK_DEV, DG), 1.0, 6.0, ((0, 4), (1, 8))),
        "gen_gain": jnp.clip(1.0 + 0.1 * jax.random.normal(splits[1], (DG,), jnp.float32), 0.5, 1.5),
        "head_weight": gaussian(splits[2], (DG, LAT), DG ** -0.5, 0.125),
        "noise": gaussian(splits[3], (N_SEQ, TOK_DEV, LAT), 1.0, 6.0, ((0, 4), (1, 8)), jnp.float32),
        "timestep": jax.random.randint(splits[4], (1,), 20, 981).astype(jnp.int32),
        "stream": draw_stream(jax.random.fold_in(splits[12], 71), 0),
        "patch_weight": gaussian(splits[6], (LAT, D_S), LAT ** -0.5, 0.75, ((1, 2),)),
        "conditions": gaussian(splits[7], (N_GROUP, D_S), 1.0, 6.0, ((0, 4), (1, 2)), jnp.float32),
        "teacher_qkv": gaussian(splits[8], (D_S, 3, HEADS, HEAD_DIM), D_S ** -0.5, 0.078125, ((0, 2), (2, 4))),
        "teacher_out": gaussian(splits[9], (HEADS, HEAD_DIM, LAT), (HEADS * HEAD_DIM) ** -0.5, 0.25, ((0, 4),)),
        "fake_qkv": gaussian(splits[10], (D_S, 3, HEADS, HEAD_DIM), D_S ** -0.5, 0.078125, ((0, 2), (2, 4))),
        "fake_out": gaussian(splits[11], (HEADS, HEAD_DIM, LAT), (HEADS * HEAD_DIM) ** -0.5, 0.25, ((0, 4),)),
    }


guidance = 3.0
eps = 1e-06

def velocity(base, cond_row, qkv_weight, out_weight):
    rows = base.shape[0]
    ds_loc = D_S // N_MP
    width = 3 * HEADS * HEAD_DIM
    layer_in = (base + cond_row[None, :]).astype(jnp.bfloat16)
    slices = layer_in.reshape(rows, N_MP, ds_loc).transpose(1, 0, 2)
    weights = qkv_weight.reshape(N_MP, ds_loc, width)

    def add_slice(total, pair):
        part = jnp.dot(pair[0], pair[1], preferred_element_type=jnp.float32).astype(jnp.bfloat16)
        part = lax.optimization_barrier(part)
        return (total + part.astype(jnp.float32), None)
    summed, _ = lax.scan(add_slice, jnp.zeros((rows, width), jnp.float32), (slices, weights))
    qkv = summed.astype(jnp.bfloat16).reshape(rows, 3, HEADS, HEAD_DIM).transpose(2, 1, 0, 3)

    def one_head(pack):
        triple, out_h = pack
        scores = jnp.dot(triple[0], triple[1].T, preferred_element_type=jnp.float32) / jnp.sqrt(jnp.float32(HEAD_DIM))
        top = lax.optimization_barrier(jnp.max(scores, axis=-1, keepdims=True))
        expo = jnp.exp(scores - top)
        probs = (expo / lax.optimization_barrier(jnp.sum(expo, axis=-1, keepdims=True))).astype(jnp.bfloat16)
        heads = jnp.dot(probs, triple[2], preferred_element_type=jnp.float32).astype(jnp.bfloat16)
        return jnp.dot(heads, out_h, preferred_element_type=jnp.float32)
    terms = lax.map(one_head, (qkv, out_weight))
    return lax.optimization_barrier(jnp.sum(terms, axis=0))

def reference(gen_hidden, gen_gain, head_weight, noise, timestep, stream, patch_weight, conditions, teacher_qkv, teacher_out, fake_qkv, fake_out):
    total = N_SEQ * TOK_DEV
    hidden = gen_hidden.reshape(total, DG).astype(jnp.float32)
    rms = 1.0 / jnp.sqrt(lax.optimization_barrier(jnp.mean(hidden * hidden, axis=-1, keepdims=True)) + eps)
    normed = (hidden * rms * gen_gain[None, :]).astype(jnp.bfloat16)
    clean = jnp.dot(normed, head_weight, preferred_element_type=jnp.float32)
    sigma = timestep[0].astype(jnp.float32) / 1000.0
    noised = ((1.0 - sigma) * clean + sigma * noise.reshape(total, LAT)).astype(jnp.bfloat16)
    base = stream.reshape(total, D_S).astype(jnp.float32) + jnp.dot(noised, patch_weight, preferred_element_type=jnp.float32)
    fake_vel = velocity(base, conditions[0], fake_qkv, fake_out)
    cond_vel = velocity(base, conditions[1], teacher_qkv, teacher_out)
    free_vel = velocity(base, conditions[2], teacher_qkv, teacher_out)
    score_gap = fake_vel - guidance * cond_vel + (guidance - 1.0) * free_vel
    gap_in = score_gap.astype(jnp.bfloat16)
    grad_normed = jnp.dot(gap_in, head_weight.T, preferred_element_type=jnp.float32)
    scaled = hidden * rms
    grad_gain = grad_normed * gen_gain[None, :]
    grad_hidden = rms * (grad_gain - scaled * lax.optimization_barrier(jnp.mean(scaled * grad_gain, axis=-1, keepdims=True)))
    return (score_gap.reshape(N_SEQ, TOK_DEV, LAT), grad_hidden.astype(jnp.bfloat16).reshape(N_SEQ, TOK_DEV, DG))
```

```python
import functools

import jax
import jax.numpy as jnp
from jax import lax
from jax.experimental import pallas as pl
from jax.experimental.pallas import tpu as pltpu
from jax.sharding import PartitionSpec as P

guidance = 3.0
eps = 1e-06
MESH = pl.DeviceIdType.MESH
F32 = jnp.float32
BF16 = jnp.bfloat16
EVALS = 3


def kernel(
    sizes,
    hid_ref,
    gain_ref,
    head_t_ref,
    noise_ref,
    time_ref,
    stream_ref,
    patch_ref,
    cond_ref,
    teacher_ref,
    teacher_out_ref,
    fake_ref,
    fake_out_ref,
    gap_ref,
    grad_ref,
    latents,
    rows,
    conds,
    w_fake,
    w_teach,
    part_out,
    part_in,
    keys_vals,
    vel_out,
    vel_in,
    local_sem,
    lat_send,
    lat_recv,
    cond_send,
    cond_recv,
    row_send,
    row_recv,
    part_send,
    part_recv,
    kv_send,
    kv_recv,
    vel_send,
    vel_recv,
):
    n_group, n_seq, n_mp, n_chunk = sizes
    g = lax.axis_index("group")
    s = lax.axis_index("seq")
    m = lax.axis_index("mp")
    per_dev = hid_ref.shape[1]
    ds_loc = stream_ref.shape[2]
    share = n_mp * per_dev
    tokens = n_seq * share
    queries = n_seq * per_dev
    head_dim = teacher_ref.shape[2]
    chunk = ds_loc // n_chunk

    def at_seq(d):
        return lax.rem(s + d, n_seq)

    def at_mp(d):
        return lax.rem(m + d, n_mp)

    def at_group(d):
        return lax.rem(g + d, n_group)

    plane = [(ds, dm) for ds in range(n_seq) for dm in range(n_mp) if ds or dm]

    def push(src, dst, send, recv, device):
        copy = pltpu.make_async_remote_copy(
            src_ref=src, dst_ref=dst, send_sem=send, recv_sem=recv, device_id=device, device_id_type=MESH
        )
        copy.start()
        return copy

    barrier = pltpu.get_barrier_semaphore()
    for ds, dm in plane:
        pl.semaphore_signal(barrier, inc=1, device_id=(g, at_seq(ds), at_mp(dm)), device_id_type=MESH)
    for d in range(1, n_group):
        pl.semaphore_signal(barrier, inc=1, device_id=(at_group(d), s, m), device_id_type=MESH)

    my_rows = pl.ds(pl.multiple_of(g * share, share), share)
    own = [
        pltpu.make_async_copy(stream_ref.at[0, my_rows, :], rows.at[s], local_sem.at[0]),
        pltpu.make_async_copy(cond_ref, conds.at[g], local_sem.at[1]),
    ]
    for j in range(3):
        cols = pl.ds(j * head_dim, head_dim)
        own.append(pltpu.make_async_copy(fake_ref.at[j], w_fake.at[:, cols], local_sem.at[2 + j]))
        own.append(pltpu.make_async_copy(teacher_ref.at[j], w_teach.at[:, cols], local_sem.at[5 + j]))
    for copy in own:
        copy.start()

    hidden = hid_ref[0].astype(F32)
    gain = gain_ref[...]
    rms = 1.0 / jnp.sqrt(jnp.mean(hidden * hidden, axis=-1, keepdims=True) + eps)
    normed = (hidden * rms * gain).astype(BF16)
    clean = lax.dot_general(normed, head_t_ref[...], (((1,), (1,)), ((), ())), preferred_element_type=F32)
    sigma = jnp.full(clean.shape, time_ref[0], jnp.int32).astype(F32) / 1000.0
    noised = ((1.0 - sigma) * clean + sigma * noise_ref[0]).astype(BF16)
    latents[s, m] = noised.astype(F32)

    pl.semaphore_wait(barrier, len(plane) + n_group - 1)

    lat_copies = []
    for i, (ds, dm) in enumerate(plane):
        lat_copies.append(
            push(latents.at[s, m], latents.at[s, m], lat_send.at[i], lat_recv.at[i], (g, at_seq(ds), at_mp(dm)))
        )
    cond_copies = []
    row_copies = []
    for c in range(n_chunk):
        cols = pl.ds(c * chunk, chunk)
        group_of = []
        for d in range(1, n_seq):
            group_of.append(
                push(
                    stream_ref.at[0, my_rows, cols],
                    rows.at[s, :, cols],
                    row_send.at[c, d - 1],
                    row_recv.at[c, d - 1],
                    (g, at_seq(d), m),
                )
            )
        row_copies.append(group_of)
        if c == 0:
            for d in range(1, n_group):
                cond_copies.append(
                    push(cond_ref, conds.at[g], cond_send.at[d - 1], cond_recv.at[d - 1], (at_group(d), s, m))
                )

    for copy in lat_copies:
        copy.wait_recv()
    lat_all = latents[...].reshape(tokens, -1).astype(BF16)
    for copy in own:
        copy.wait()
    for copy in cond_copies:
        copy.wait_recv()

    acc_fake = None
    acc_teach = None
    for c in range(n_chunk):
        cols = pl.ds(c * chunk, chunk)
        for copy in row_copies[c]:
            copy.wait_recv()
        base = rows[:, :, cols].reshape(tokens, chunk).astype(F32) + jnp.dot(
            lat_all, patch_ref[:, cols], preferred_element_type=F32
        )
        layer = [(base + conds[e, :, cols]).astype(BF16) for e in range(EVALS)]
        fake = jnp.dot(layer[0], w_fake[cols, :], preferred_element_type=F32)
        teach = jnp.dot(jnp.concatenate(layer[1:], axis=0), w_teach[cols, :], preferred_element_type=F32)
        acc_fake = fake if c == 0 else acc_fake + fake
        acc_teach = teach if c == 0 else acc_teach + teach

    partial = [acc_fake, acc_teach[:tokens], acc_teach[tokens:]]
    part_copies = []
    for e in range(EVALS):
        q_part = partial[e][:, :head_dim].reshape(n_seq, n_mp, per_dev, head_dim)
        k_part = partial[e][:, head_dim : 2 * head_dim].astype(BF16)
        v_part = partial[e][:, 2 * head_dim :].astype(BF16)
        for k in range(n_mp):
            part_out[e, k, :tokens] = k_part
            part_out[e, k, tokens : 2 * tokens] = v_part
            part_out[e, k, 2 * tokens :] = q_part[:, k].reshape(queries, head_dim).astype(BF16)
        part_copies.append(
            [
                push(
                    part_out.at[e, at_mp(d)],
                    part_in.at[e, d - 1],
                    part_send.at[e, d - 1],
                    part_recv.at[e, d - 1],
                    (g, s, at_mp(d)),
                )
                for d in range(1, n_mp)
            ]
        )

    kv_copies = []
    queries_of = []
    for e in range(EVALS):
        total = part_out[e, m].astype(F32)
        for d in range(1, n_mp):
            part_copies[e][d - 1].wait_recv()
            total = total + part_in[e, d - 1].astype(F32)
        total = total.astype(BF16)
        keys_vals[e, g] = total[: 2 * tokens]
        queries_of.append(total[2 * tokens :])
        kv_copies.append(
            [
                push(
                    keys_vals.at[e, g],
                    keys_vals.at[e, g],
                    kv_send.at[e, d - 1],
                    kv_recv.at[e, d - 1],
                    (at_group(d), s, m),
                )
                for d in range(1, n_group)
            ]
        )

    coeff = (1.0, -guidance, guidance - 1.0)
    velocity = None
    for e in range(EVALS):
        for copy in kv_copies[e]:
            copy.wait_recv()
        keys = keys_vals[e, :, :tokens].reshape(n_group * tokens, head_dim)
        values = keys_vals[e, :, tokens:].reshape(n_group * tokens, head_dim)
        scores = lax.dot_general(
            queries_of[e], keys, (((1,), (1,)), ((), ())), preferred_element_type=F32
        ) / jnp.sqrt(F32(head_dim))
        top = jnp.max(scores, axis=-1, keepdims=True)
        expo = jnp.exp(scores - top)
        probs = (expo / jnp.sum(expo, axis=-1, keepdims=True)).astype(BF16)
        heads = jnp.dot(probs, values, preferred_element_type=F32).astype(BF16)
        out_t = fake_out_ref[0] if e == 0 else teacher_out_ref[0]
        term = coeff[e] * lax.dot_general(heads, out_t, (((1,), (1,)), ((), ())), preferred_element_type=F32)
        velocity = term if e == 0 else velocity + term

    vel_out[...] = velocity.reshape(n_seq, per_dev, -1)
    vel_copies = [
        push(vel_out.at[at_seq(d)], vel_in.at[s], vel_send.at[d - 1], vel_recv.at[d - 1], (g, at_seq(d), m))
        for d in range(1, n_seq)
    ]
    vel_in[s] = vel_out[s]
    scaled = hidden * rms
    for copy in vel_copies:
        copy.wait_recv()
    gap = vel_in[0]
    for k in range(1, n_seq):
        gap = gap + vel_in[k]
    gap_ref[0] = gap
    grad_normed = jnp.dot(gap.astype(BF16), head_t_ref[...], preferred_element_type=F32)
    grad_gain = grad_normed * gain
    grad = rms * (grad_gain - scaled * jnp.mean(scaled * grad_gain, axis=-1, keepdims=True))
    grad_ref[0] = grad.astype(BF16)

    for copy in lat_copies + cond_copies + vel_copies:
        copy.wait_send()
    for copies in row_copies + part_copies + kv_copies:
        for copy in copies:
            copy.wait_send()


def fused(
    gen_hidden,
    gen_gain,
    head_weight,
    noise,
    timestep,
    stream,
    patch_weight,
    conditions,
    teacher_qkv,
    teacher_out,
    fake_qkv,
    fake_out,
):
    n_group = lax.axis_size("group")
    n_seq = lax.axis_size("seq")
    n_mp = lax.axis_size("mp")
    per_dev = gen_hidden.shape[1]
    lat = head_weight.shape[1]
    ds_loc = stream.shape[2]
    head_dim = teacher_qkv.shape[3]
    share = n_mp * per_dev
    tokens = n_seq * share
    queries = n_seq * per_dev
    width = 3 * head_dim
    n_chunk = ds_loc // 512
    packed = 2 * tokens + queries
    n_plane = n_seq * n_mp - 1
    vmem = pl.BlockSpec(memory_space=pltpu.VMEM)
    hbm = pl.BlockSpec(memory_space=pl.ANY)
    smem = pl.BlockSpec(memory_space=pltpu.SMEM)
    dma = pltpu.SemaphoreType.DMA
    return pl.pallas_call(
        functools.partial(kernel, (n_group, n_seq, n_mp, n_chunk)),
        out_shape=(
            jax.ShapeDtypeStruct((1, per_dev, lat), F32),
            jax.ShapeDtypeStruct(gen_hidden.shape, BF16),
        ),
        in_specs=[vmem, vmem, vmem, vmem, smem, hbm, vmem, vmem, hbm, vmem, hbm, vmem],
        out_specs=(vmem, vmem),
        scratch_shapes=[
            pltpu.VMEM((n_seq, n_mp, per_dev, lat), F32),
            pltpu.VMEM((n_seq, share, ds_loc), BF16),
            pltpu.VMEM((n_group, 1, ds_loc), F32),
            pltpu.VMEM((ds_loc, width), BF16),
            pltpu.VMEM((ds_loc, width), BF16),
            pltpu.VMEM((EVALS, n_mp, packed, head_dim), BF16),
            pltpu.VMEM((EVALS, n_mp - 1, packed, head_dim), BF16),
            pltpu.VMEM((EVALS, n_group, 2 * tokens, head_dim), BF16),
            pltpu.VMEM((n_seq, per_dev, lat), F32),
            pltpu.VMEM((n_seq, per_dev, lat), F32),
            dma((8,)),
            dma((n_plane,)),
            dma((n_plane,)),
            dma((n_group - 1,)),
            dma((n_group - 1,)),
            dma((n_chunk, n_seq - 1)),
            dma((n_chunk, n_seq - 1)),
            dma((EVALS, n_mp - 1)),
            dma((EVALS, n_mp - 1)),
            dma((EVALS, n_group - 1)),
            dma((EVALS, n_group - 1)),
            dma((n_seq - 1,)),
            dma((n_seq - 1,)),
        ],
        compiler_params=pltpu.CompilerParams(
            collective_id=0, has_side_effects=True, vmem_limit_bytes=40 * 1024 * 1024
        ),
    )(
        gen_hidden,
        gen_gain.reshape(1, -1),
        head_weight.T,
        noise,
        timestep,
        stream,
        patch_weight,
        conditions,
        teacher_qkv[:, :, 0, :].transpose(1, 0, 2),
        teacher_out.transpose(0, 2, 1),
        fake_qkv[:, :, 0, :].transpose(1, 0, 2),
        fake_out.transpose(0, 2, 1),
    )


def local(
    gen_hidden,
    gen_gain,
    head_weight,
    noise,
    timestep,
    stream,
    patch_weight,
    conditions,
    teacher_qkv,
    teacher_out,
    fake_qkv,
    fake_out,
):
    n_group = lax.axis_size("group")
    n_seq = lax.axis_size("seq")
    n_mp = lax.axis_size("mp")
    group_id = lax.axis_index("group")
    tok_dev = stream.shape[1]
    ds_loc = stream.shape[2]
    head_dim = teacher_qkv.shape[3]
    per_dev = gen_hidden.shape[1]
    width = 3 * head_dim
    hidden = gen_hidden[0].astype(jnp.float32)
    rms = 1.0 / jnp.sqrt(jnp.mean(hidden * hidden, axis=-1, keepdims=True) + eps)
    normed = (hidden * rms * gen_gain[None, :]).astype(jnp.bfloat16)
    clean = jnp.dot(normed, head_weight, preferred_element_type=jnp.float32)
    sigma = timestep[0].astype(jnp.float32) / 1000.0
    noised = ((1.0 - sigma) * clean + sigma * noise[0]).astype(jnp.bfloat16)
    is_fake = group_id == 0
    qkv_weight = jnp.where(is_fake, fake_qkv, teacher_qkv).reshape(ds_loc, width)
    out_weight = jnp.where(is_fake, fake_out, teacher_out)[0]
    coeff = jnp.where(
        group_id == 0,
        1.0,
        jnp.where(group_id == 1, -guidance, jnp.where(group_id == 2, guidance - 1.0, 0.0)),
    )
    cond_row = conditions[0][None, None, :]
    block_lat = lax.all_gather(noised, ("group", "mp"), axis=0, tiled=True)
    embedded = jnp.dot(block_lat, patch_weight, preferred_element_type=jnp.float32)
    rows = (stream[0].astype(jnp.float32) + embedded + cond_row[0]).astype(jnp.bfloat16)[None]
    queries_count = n_group * n_seq * per_dev
    piece = lax.all_gather(rows, "seq", axis=0, tiled=True)
    product = jnp.dot(piece.reshape(-1, ds_loc), qkv_weight, preferred_element_type=jnp.float32)
    partial_value = product.reshape(piece.shape[0], tok_dev, width)
    kv_part = partial_value[:, :, head_dim:].reshape(n_seq * tok_dev, 2 * head_dim)
    keys_vals = lax.psum(kv_part.astype(jnp.bfloat16), "mp")
    query_part = partial_value[:, :, :head_dim].reshape(n_seq, n_group, n_mp, per_dev, head_dim)
    query_part = query_part.transpose(2, 1, 0, 3, 4).reshape(n_mp * queries_count, head_dim)
    queries = lax.psum_scatter(
        query_part.astype(jnp.bfloat16), "mp", scatter_dimension=0, tiled=True
    )
    keys = keys_vals[:, :head_dim]
    values = keys_vals[:, head_dim:]
    scores = jnp.dot(queries, keys.T, preferred_element_type=jnp.float32) / jnp.sqrt(
        jnp.float32(head_dim)
    )
    top = jnp.max(scores, axis=-1, keepdims=True)
    expo = jnp.exp(scores - top)
    probs = (expo / jnp.sum(expo, axis=-1, keepdims=True)).astype(jnp.bfloat16)
    heads = jnp.dot(probs, values, preferred_element_type=jnp.float32).astype(jnp.bfloat16)
    weighted = coeff * jnp.dot(heads, out_weight, preferred_element_type=jnp.float32)
    score_gap = lax.psum_scatter(weighted, ("group", "seq"), scatter_dimension=0, tiled=True)
    gap_in = score_gap.astype(jnp.bfloat16)
    grad_normed = jnp.dot(gap_in, head_weight.T, preferred_element_type=jnp.float32)
    scaled = hidden * rms
    grad_gain = grad_normed * gen_gain[None, :]
    grad_hidden = rms * (grad_gain - scaled * jnp.mean(scaled * grad_gain, axis=-1, keepdims=True))
    return (score_gap[None], grad_hidden.astype(jnp.bfloat16)[None])


def solution(mesh):
    placed = (
        P("seq", ("group", "mp"), None),
        P(),
        P(),
        P("seq", ("group", "mp"), None),
        P(),
        P("seq", None, "mp"),
        P(None, "mp"),
        P("group", "mp"),
        P("mp", None, "seq", None),
        P("seq", None, None),
        P("mp", None, "seq", None),
        P("seq", None, None),
    )
    n_group, n_seq, n_mp = mesh.shape["group"], mesh.shape["seq"], mesh.shape["mp"]

    def part(*arrays):
        per_dev, ds_loc = arrays[0].shape[1], arrays[5].shape[2]
        tiled = per_dev % 8 == 0 and n_mp * per_dev % 16 == 0 and n_seq * per_dev % 16 == 0
        small = n_group > 1 and n_seq > 1 and n_mp > 1 and n_group >= EVALS
        if tiled and small and ds_loc % 512 == 0:
            return fused(*arrays)
        return local(*arrays)

    return jax.shard_map(
        part,
        mesh=mesh,
        in_specs=placed,
        out_specs=(P("seq", ("group", "mp"), None), P("seq", ("group", "mp"), None)),
        check_vma=False,
    )
```

```python
import functools

import jax
import jax.numpy as jnp
from jax import lax
from jax.experimental import pallas as pl
from jax.experimental.pallas import tpu as pltpu
from jax.sharding import PartitionSpec as P

guidance = 3.0
eps = 1e-06
MESH = pl.DeviceIdType.MESH
F32 = jnp.float32
BF16 = jnp.bfloat16
EVALS = 3


def kernel(
    sizes,
    hid_hbm,
    gain_hbm,
    head_t_hbm,
    noise_hbm,
    time_ref,
    stream_ref,
    patch_hbm,
    cond_ref,
    teacher_ref,
    teacher_out_hbm,
    fake_ref,
    fake_out_hbm,
    gap_ref,
    grad_ref,
    hid_ref,
    gain_ref,
    head_t_ref,
    noise_ref,
    patch_ref,
    teacher_out_ref,
    fake_out_ref,
    latents,
    rows,
    conds,
    w_fake,
    w_teach,
    part_out,
    part_in,
    keys_vals,
    vel_out,
    vel_in,
    small_sem,
    local_sem,
    lat_send,
    lat_recv,
    cond_send,
    cond_recv,
    row_send,
    row_recv,
    part_send,
    part_recv,
    kv_send,
    kv_recv,
    vel_send,
    vel_recv,
):
    n_group, n_seq, n_mp, n_chunk = sizes
    g = lax.axis_index("group")
    s = lax.axis_index("seq")
    m = lax.axis_index("mp")
    per_dev = hid_ref.shape[1]
    ds_loc = stream_ref.shape[2]
    share = n_mp * per_dev
    tokens = n_seq * share
    queries = n_seq * per_dev
    head_dim = teacher_ref.shape[2]
    chunk = ds_loc // n_chunk

    def at_seq(d):
        return lax.rem(s + d, n_seq)

    def at_mp(d):
        return lax.rem(m + d, n_mp)

    def at_group(d):
        return lax.rem(g + d, n_group)

    plane = [(ds, dm) for ds in range(n_seq) for dm in range(n_mp) if ds or dm]

    def push(src, dst, send, recv, device):
        copy = pltpu.make_async_remote_copy(
            src_ref=src, dst_ref=dst, send_sem=send, recv_sem=recv, device_id=device, device_id_type=MESH
        )
        copy.start()
        return copy

    barrier = pltpu.get_barrier_semaphore()
    for ds, dm in plane:
        pl.semaphore_signal(barrier, inc=1, device_id=(g, at_seq(ds), at_mp(dm)), device_id_type=MESH)
    for d in range(1, n_group):
        pl.semaphore_signal(barrier, inc=1, device_id=(at_group(d), s, m), device_id_type=MESH)

    my_rows = pl.ds(pl.multiple_of(g * share, share), share)
    small = [
        pltpu.make_async_copy(src, dst, small_sem.at[i])
        for i, (src, dst) in enumerate(
            (
                (hid_hbm, hid_ref),
                (gain_hbm, gain_ref),
                (head_t_hbm, head_t_ref),
                (noise_hbm, noise_ref),
                (patch_hbm, patch_ref),
                (teacher_out_hbm, teacher_out_ref),
                (fake_out_hbm, fake_out_ref),
            )
        )
    ]
    own = [
        pltpu.make_async_copy(stream_ref.at[0, my_rows, :], rows.at[s], local_sem.at[0]),
        pltpu.make_async_copy(cond_ref, conds.at[g], local_sem.at[1]),
    ]
    for j in range(3):
        cols = pl.ds(j * head_dim, head_dim)
        own.append(pltpu.make_async_copy(fake_ref.at[j], w_fake.at[:, cols], local_sem.at[2 + j]))
        own.append(pltpu.make_async_copy(teacher_ref.at[j], w_teach.at[:, cols], local_sem.at[5 + j]))
    for copy in small[:4] + own[:2] + small[4:] + own[2:]:
        copy.start()
    for copy in small[:4]:
        copy.wait()

    hidden = hid_ref[0].astype(F32)
    gain = gain_ref[...]
    rms = 1.0 / jnp.sqrt(jnp.mean(hidden * hidden, axis=-1, keepdims=True) + eps)
    normed = (hidden * rms * gain).astype(BF16)
    clean = lax.dot_general(normed, head_t_ref[...], (((1,), (1,)), ((), ())), preferred_element_type=F32)
    sigma = jnp.full(clean.shape, time_ref[0], jnp.int32).astype(F32) / 1000.0
    noised = ((1.0 - sigma) * clean + sigma * noise_ref[0]).astype(BF16)
    latents[s, m] = noised.astype(F32)

    pl.semaphore_wait(barrier, len(plane) + n_group - 1)

    lat_copies = []
    for i, (ds, dm) in enumerate(plane):
        lat_copies.append(
            push(latents.at[s, m], latents.at[s, m], lat_send.at[i], lat_recv.at[i], (g, at_seq(ds), at_mp(dm)))
        )
    cond_copies = []
    row_copies = []
    for c in range(n_chunk):
        cols = pl.ds(c * chunk, chunk)
        group_of = []
        for d in range(1, n_seq):
            group_of.append(
                push(
                    stream_ref.at[0, my_rows, cols],
                    rows.at[s, :, cols],
                    row_send.at[c, d - 1],
                    row_recv.at[c, d - 1],
                    (g, at_seq(d), m),
                )
            )
        row_copies.append(group_of)
        if c == 0:
            for d in range(1, n_group):
                cond_copies.append(
                    push(cond_ref, conds.at[g], cond_send.at[d - 1], cond_recv.at[d - 1], (at_group(d), s, m))
                )

    for copy in lat_copies:
        copy.wait_recv()
    lat_all = latents[...].reshape(tokens, -1).astype(BF16)
    for copy in own + small[4:]:
        copy.wait()
    for copy in cond_copies:
        copy.wait_recv()

    acc_fake = None
    acc_teach = None
    for c in range(n_chunk):
        cols = pl.ds(c * chunk, chunk)
        for copy in row_copies[c]:
            copy.wait_recv()
        base = rows[:, :, cols].reshape(tokens, chunk).astype(F32) + jnp.dot(
            lat_all, patch_ref[:, cols], preferred_element_type=F32
        )
        layer = [(base + conds[e, :, cols]).astype(BF16) for e in range(EVALS)]
        fake = jnp.dot(layer[0], w_fake[cols, :], preferred_element_type=F32)
        teach = jnp.dot(jnp.concatenate(layer[1:], axis=0), w_teach[cols, :], preferred_element_type=F32)
        acc_fake = fake if c == 0 else acc_fake + fake
        acc_teach = teach if c == 0 else acc_teach + teach

    partial = [acc_fake, acc_teach[:tokens], acc_teach[tokens:]]
    part_copies = []
    for e in range(EVALS):
        q_part = partial[e][:, :head_dim].reshape(n_seq, n_mp, per_dev, head_dim)
        k_part = partial[e][:, head_dim : 2 * head_dim].astype(BF16)
        v_part = partial[e][:, 2 * head_dim :].astype(BF16)
        for k in range(n_mp):
            part_out[e, k, :tokens] = k_part
            part_out[e, k, tokens : 2 * tokens] = v_part
            part_out[e, k, 2 * tokens :] = q_part[:, k].reshape(queries, head_dim).astype(BF16)
        part_copies.append(
            [
                push(
                    part_out.at[e, at_mp(d)],
                    part_in.at[e, d - 1],
                    part_send.at[e, d - 1],
                    part_recv.at[e, d - 1],
                    (g, s, at_mp(d)),
                )
                for d in range(1, n_mp)
            ]
        )

    kv_copies = []
    queries_of = []
    for e in range(EVALS):
        total = part_out[e, m].astype(F32)
        for d in range(1, n_mp):
            part_copies[e][d - 1].wait_recv()
            total = total + part_in[e, d - 1].astype(F32)
        total = total.astype(BF16)
        keys_vals[e, g] = total[: 2 * tokens]
        queries_of.append(total[2 * tokens :])
        kv_copies.append(
            [
                push(
                    keys_vals.at[e, g],
                    keys_vals.at[e, g],
                    kv_send.at[e, d - 1],
                    kv_recv.at[e, d - 1],
                    (at_group(d), s, m),
                )
                for d in range(1, n_group)
            ]
        )

    coeff = (1.0, -guidance, guidance - 1.0)
    velocity = None
    for e in range(EVALS):
        for copy in kv_copies[e]:
            copy.wait_recv()
        keys = keys_vals[e, :, :tokens].reshape(n_group * tokens, head_dim)
        values = keys_vals[e, :, tokens:].reshape(n_group * tokens, head_dim)
        scores = lax.dot_general(
            queries_of[e], keys, (((1,), (1,)), ((), ())), preferred_element_type=F32
        ) / jnp.sqrt(F32(head_dim))
        top = jnp.max(scores, axis=-1, keepdims=True)
        expo = jnp.exp(scores - top)
        probs = (expo / jnp.sum(expo, axis=-1, keepdims=True)).astype(BF16)
        heads = jnp.dot(probs, values, preferred_element_type=F32).astype(BF16)
        out_t = fake_out_ref[0] if e == 0 else teacher_out_ref[0]
        term = coeff[e] * lax.dot_general(heads, out_t, (((1,), (1,)), ((), ())), preferred_element_type=F32)
        velocity = term if e == 0 else velocity + term

    vel_out[...] = velocity.reshape(n_seq, per_dev, -1)
    vel_copies = [
        push(vel_out.at[at_seq(d)], vel_in.at[s], vel_send.at[d - 1], vel_recv.at[d - 1], (g, at_seq(d), m))
        for d in range(1, n_seq)
    ]
    vel_in[s] = vel_out[s]
    scaled = hidden * rms
    for copy in vel_copies:
        copy.wait_recv()
    gap = vel_in[0]
    for k in range(1, n_seq):
        gap = gap + vel_in[k]
    gap_ref[0] = gap
    grad_normed = jnp.dot(gap.astype(BF16), head_t_ref[...], preferred_element_type=F32)
    grad_gain = grad_normed * gain
    grad = rms * (grad_gain - scaled * jnp.mean(scaled * grad_gain, axis=-1, keepdims=True))
    grad_ref[0] = grad.astype(BF16)

    for copy in lat_copies + cond_copies + vel_copies:
        copy.wait_send()
    for copies in row_copies + part_copies + kv_copies:
        for copy in copies:
            copy.wait_send()


def fused(
    gen_hidden,
    gen_gain,
    head_weight,
    noise,
    timestep,
    stream,
    patch_weight,
    conditions,
    teacher_qkv,
    teacher_out,
    fake_qkv,
    fake_out,
):
    n_group = lax.axis_size("group")
    n_seq = lax.axis_size("seq")
    n_mp = lax.axis_size("mp")
    per_dev = gen_hidden.shape[1]
    lat = head_weight.shape[1]
    ds_loc = stream.shape[2]
    head_dim = teacher_qkv.shape[3]
    share = n_mp * per_dev
    tokens = n_seq * share
    queries = n_seq * per_dev
    width = 3 * head_dim
    n_chunk = ds_loc // 512
    packed = 2 * tokens + queries
    n_plane = n_seq * n_mp - 1
    vmem = pl.BlockSpec(memory_space=pltpu.VMEM)
    hbm = pl.BlockSpec(memory_space=pltpu.HBM)
    smem = pl.BlockSpec(memory_space=pltpu.SMEM)
    dma = pltpu.SemaphoreType.DMA
    return pl.pallas_call(
        functools.partial(kernel, (n_group, n_seq, n_mp, n_chunk)),
        out_shape=(
            jax.ShapeDtypeStruct((1, per_dev, lat), F32),
            jax.ShapeDtypeStruct(gen_hidden.shape, BF16),
        ),
        in_specs=[hbm] * 4 + [smem] + [hbm] * 7,
        out_specs=(vmem, vmem),
        scratch_shapes=[
            pltpu.VMEM(gen_hidden.shape, BF16),
            pltpu.VMEM((1, gen_hidden.shape[2]), F32),
            pltpu.VMEM(head_weight.shape[::-1], BF16),
            pltpu.VMEM(noise.shape, F32),
            pltpu.VMEM(patch_weight.shape, BF16),
            pltpu.VMEM((1, lat, head_dim), BF16),
            pltpu.VMEM((1, lat, head_dim), BF16),
            pltpu.VMEM((n_seq, n_mp, per_dev, lat), F32),
            pltpu.VMEM((n_seq, share, ds_loc), BF16),
            pltpu.VMEM((n_group, 1, ds_loc), F32),
            pltpu.VMEM((ds_loc, width), BF16),
            pltpu.VMEM((ds_loc, width), BF16),
            pltpu.VMEM((EVALS, n_mp, packed, head_dim), BF16),
            pltpu.VMEM((EVALS, n_mp - 1, packed, head_dim), BF16),
            pltpu.VMEM((EVALS, n_group, 2 * tokens, head_dim), BF16),
            pltpu.VMEM((n_seq, per_dev, lat), F32),
            pltpu.VMEM((n_seq, per_dev, lat), F32),
            dma((7,)),
            dma((8,)),
            dma((n_plane,)),
            dma((n_plane,)),
            dma((n_group - 1,)),
            dma((n_group - 1,)),
            dma((n_chunk, n_seq - 1)),
            dma((n_chunk, n_seq - 1)),
            dma((EVALS, n_mp - 1)),
            dma((EVALS, n_mp - 1)),
            dma((EVALS, n_group - 1)),
            dma((EVALS, n_group - 1)),
            dma((n_seq - 1,)),
            dma((n_seq - 1,)),
        ],
        compiler_params=pltpu.CompilerParams(
            collective_id=0, has_side_effects=True, vmem_limit_bytes=56 * 1024 * 1024
        ),
    )(
        gen_hidden,
        gen_gain.reshape(1, -1),
        head_weight.T,
        noise,
        timestep,
        stream,
        patch_weight,
        conditions,
        teacher_qkv[:, :, 0, :].transpose(1, 0, 2),
        teacher_out.transpose(0, 2, 1),
        fake_qkv[:, :, 0, :].transpose(1, 0, 2),
        fake_out.transpose(0, 2, 1),
    )


def local(
    gen_hidden,
    gen_gain,
    head_weight,
    noise,
    timestep,
    stream,
    patch_weight,
    conditions,
    teacher_qkv,
    teacher_out,
    fake_qkv,
    fake_out,
):
    n_group = lax.axis_size("group")
    n_seq = lax.axis_size("seq")
    n_mp = lax.axis_size("mp")
    group_id = lax.axis_index("group")
    tok_dev = stream.shape[1]
    ds_loc = stream.shape[2]
    head_dim = teacher_qkv.shape[3]
    per_dev = gen_hidden.shape[1]
    width = 3 * head_dim
    hidden = gen_hidden[0].astype(jnp.float32)
    rms = 1.0 / jnp.sqrt(jnp.mean(hidden * hidden, axis=-1, keepdims=True) + eps)
    normed = (hidden * rms * gen_gain[None, :]).astype(jnp.bfloat16)
    clean = jnp.dot(normed, head_weight, preferred_element_type=jnp.float32)
    sigma = timestep[0].astype(jnp.float32) / 1000.0
    noised = ((1.0 - sigma) * clean + sigma * noise[0]).astype(jnp.bfloat16)
    is_fake = group_id == 0
    qkv_weight = jnp.where(is_fake, fake_qkv, teacher_qkv).reshape(ds_loc, width)
    out_weight = jnp.where(is_fake, fake_out, teacher_out)[0]
    coeff = jnp.where(
        group_id == 0,
        1.0,
        jnp.where(group_id == 1, -guidance, jnp.where(group_id == 2, guidance - 1.0, 0.0)),
    )
    cond_row = conditions[0][None, None, :]
    block_lat = lax.all_gather(noised, ("group", "mp"), axis=0, tiled=True)
    embedded = jnp.dot(block_lat, patch_weight, preferred_element_type=jnp.float32)
    rows = (stream[0].astype(jnp.float32) + embedded + cond_row[0]).astype(jnp.bfloat16)[None]
    queries_count = n_group * n_seq * per_dev
    piece = lax.all_gather(rows, "seq", axis=0, tiled=True)
    product = jnp.dot(piece.reshape(-1, ds_loc), qkv_weight, preferred_element_type=jnp.float32)
    partial_value = product.reshape(piece.shape[0], tok_dev, width)
    kv_part = partial_value[:, :, head_dim:].reshape(n_seq * tok_dev, 2 * head_dim)
    keys_vals = lax.psum(kv_part.astype(jnp.bfloat16), "mp")
    query_part = partial_value[:, :, :head_dim].reshape(n_seq, n_group, n_mp, per_dev, head_dim)
    query_part = query_part.transpose(2, 1, 0, 3, 4).reshape(n_mp * queries_count, head_dim)
    queries = lax.psum_scatter(
        query_part.astype(jnp.bfloat16), "mp", scatter_dimension=0, tiled=True
    )
    keys = keys_vals[:, :head_dim]
    values = keys_vals[:, head_dim:]
    scores = jnp.dot(queries, keys.T, preferred_element_type=jnp.float32) / jnp.sqrt(
        jnp.float32(head_dim)
    )
    top = jnp.max(scores, axis=-1, keepdims=True)
    expo = jnp.exp(scores - top)
    probs = (expo / jnp.sum(expo, axis=-1, keepdims=True)).astype(jnp.bfloat16)
    heads = jnp.dot(probs, values, preferred_element_type=jnp.float32).astype(jnp.bfloat16)
    weighted = coeff * jnp.dot(heads, out_weight, preferred_element_type=jnp.float32)
    score_gap = lax.psum_scatter(weighted, ("group", "seq"), scatter_dimension=0, tiled=True)
    gap_in = score_gap.astype(jnp.bfloat16)
    grad_normed = jnp.dot(gap_in, head_weight.T, preferred_element_type=jnp.float32)
    scaled = hidden * rms
    grad_gain = grad_normed * gen_gain[None, :]
    grad_hidden = rms * (grad_gain - scaled * jnp.mean(scaled * grad_gain, axis=-1, keepdims=True))
    return (score_gap[None], grad_hidden.astype(jnp.bfloat16)[None])


def solution(mesh):
    placed = (
        P("seq", ("group", "mp"), None),
        P(),
        P(),
        P("seq", ("group", "mp"), None),
        P(),
        P("seq", None, "mp"),
        P(None, "mp"),
        P("group", "mp"),
        P("mp", None, "seq", None),
        P("seq", None, None),
        P("mp", None, "seq", None),
        P("seq", None, None),
    )
    n_group, n_seq, n_mp = mesh.shape["group"], mesh.shape["seq"], mesh.shape["mp"]

    def part(*arrays):
        per_dev, ds_loc = arrays[0].shape[1], arrays[5].shape[2]
        tiled = per_dev % 8 == 0 and n_mp * per_dev % 16 == 0 and n_seq * per_dev % 16 == 0
        small = n_group > 1 and n_seq > 1 and n_mp > 1 and n_group >= EVALS
        if tiled and small and ds_loc % 512 == 0:
            return fused(*arrays)
        return local(*arrays)

    return jax.shard_map(
        part,
        mesh=mesh,
        in_specs=placed,
        out_specs=(P("seq", ("group", "mp"), None), P("seq", ("group", "mp"), None)),
        check_vma=False,
    )
```

```python
import functools

import jax
import jax.numpy as jnp
from jax import lax
from jax.experimental import pallas as pl
from jax.experimental.pallas import tpu as pltpu
from jax.sharding import PartitionSpec as P

guidance = 3.0
eps = 1e-06
MESH = pl.DeviceIdType.MESH
F32 = jnp.float32
BF16 = jnp.bfloat16
EVALS = 3


def kernel(
    sizes,
    hid_hbm,
    gain_hbm,
    head_t_hbm,
    noise_hbm,
    time_ref,
    stream_ref,
    patch_hbm,
    cond_ref,
    teacher_ref,
    teacher_out_hbm,
    fake_ref,
    fake_out_hbm,
    gap_ref,
    grad_ref,
    hid_ref,
    gain_ref,
    head_t_ref,
    noise_ref,
    patch_ref,
    teacher_out_ref,
    fake_out_ref,
    latents,
    rows,
    conds,
    w_fake,
    w_teach,
    part_out,
    part_in,
    vel_out,
    vel_in,
    small_sem,
    local_sem,
    lat_send,
    lat_recv,
    cond_send,
    cond_recv,
    row_send,
    row_recv,
    part_send,
    part_recv,
    vel_send,
    vel_recv,
):
    n_group, n_seq, n_mp, n_chunk = sizes
    g = lax.axis_index("group")
    s = lax.axis_index("seq")
    m = lax.axis_index("mp")
    per_dev = hid_ref.shape[1]
    ds_loc = stream_ref.shape[2]
    share = n_mp * per_dev
    tokens = n_seq * share
    queries = n_seq * per_dev
    head_dim = teacher_ref.shape[2]
    chunk = ds_loc // n_chunk

    def at_seq(d):
        return lax.rem(s + d, n_seq)

    def at_mp(d):
        return lax.rem(m + d, n_mp)

    def at_group(d):
        return lax.rem(g + d, n_group)

    plane = [(ds, dm) for ds in range(n_seq) for dm in range(n_mp) if ds or dm]

    def push(src, dst, send, recv, device):
        copy = pltpu.make_async_remote_copy(
            src_ref=src, dst_ref=dst, send_sem=send, recv_sem=recv, device_id=device, device_id_type=MESH
        )
        copy.start()
        return copy

    barrier = pltpu.get_barrier_semaphore()
    for ds, dm in plane:
        pl.semaphore_signal(barrier, inc=1, device_id=(g, at_seq(ds), at_mp(dm)), device_id_type=MESH)
    cross = [(dg, ds, 0) for dg in range(1, n_group) for ds in range(n_seq)]
    cross += [(dg, 0, dm) for dg in range(1, n_group) for dm in range(1, n_mp)]
    for dg, ds, dm in cross:
        pl.semaphore_signal(
            barrier, inc=1, device_id=(at_group(dg), at_seq(ds), at_mp(dm)), device_id_type=MESH
        )

    my_rows = pl.ds(pl.multiple_of(g * share, share), share)
    small = [
        pltpu.make_async_copy(src, dst, small_sem.at[i])
        for i, (src, dst) in enumerate(
            (
                (hid_hbm, hid_ref),
                (gain_hbm, gain_ref),
                (head_t_hbm, head_t_ref),
                (noise_hbm, noise_ref),
                (patch_hbm, patch_ref),
                (teacher_out_hbm, teacher_out_ref),
                (fake_out_hbm, fake_out_ref),
            )
        )
    ]
    own = [
        pltpu.make_async_copy(stream_ref.at[0, my_rows, :], rows.at[s], local_sem.at[0]),
        pltpu.make_async_copy(cond_ref, conds.at[g], local_sem.at[1]),
    ]
    for j in range(3):
        cols = pl.ds(j * head_dim, head_dim)
        own.append(pltpu.make_async_copy(fake_ref.at[j], w_fake.at[:, cols], local_sem.at[2 + j]))
        own.append(pltpu.make_async_copy(teacher_ref.at[j], w_teach.at[:, cols], local_sem.at[5 + j]))
    for copy in small[:4] + own[:2] + small[4:] + own[2:]:
        copy.start()
    for copy in small[:4]:
        copy.wait()

    hidden = hid_ref[0].astype(F32)
    gain = gain_ref[...]
    rms = 1.0 / jnp.sqrt(jnp.mean(hidden * hidden, axis=-1, keepdims=True) + eps)
    normed = (hidden * rms * gain).astype(BF16)
    clean = lax.dot_general(normed, head_t_ref[...], (((1,), (1,)), ((), ())), preferred_element_type=F32)
    sigma = jnp.full(clean.shape, time_ref[0], jnp.int32).astype(F32) / 1000.0
    noised = ((1.0 - sigma) * clean + sigma * noise_ref[0]).astype(BF16)
    latents[s, m] = noised.astype(F32)

    pl.semaphore_wait(barrier, len(plane) + len(cross))

    lat_copies = []
    for i, (ds, dm) in enumerate(plane):
        lat_copies.append(
            push(latents.at[s, m], latents.at[s, m], lat_send.at[i], lat_recv.at[i], (g, at_seq(ds), at_mp(dm)))
        )
    cond_copies = []
    row_copies = []
    for c in range(n_chunk):
        cols = pl.ds(c * chunk, chunk)
        group_of = []
        for d in range(1, n_seq):
            group_of.append(
                push(
                    stream_ref.at[0, my_rows, cols],
                    rows.at[s, :, cols],
                    row_send.at[c, d - 1],
                    row_recv.at[c, d - 1],
                    (g, at_seq(d), m),
                )
            )
        row_copies.append(group_of)
        if c == 0:
            for d in range(1, n_group):
                cond_copies.append(
                    push(cond_ref, conds.at[g], cond_send.at[d - 1], cond_recv.at[d - 1], (at_group(d), s, m))
                )

    for copy in lat_copies:
        copy.wait_recv()
    lat_all = latents[...].reshape(tokens, -1).astype(BF16)
    for copy in own + small[4:]:
        copy.wait()
    for copy in cond_copies:
        copy.wait_recv()

    acc_fake = None
    acc_teach = None
    for c in range(n_chunk):
        cols = pl.ds(c * chunk, chunk)
        for copy in row_copies[c]:
            copy.wait_recv()
        base = rows[:, :, cols].reshape(tokens, chunk).astype(F32) + jnp.dot(
            lat_all, patch_ref[:, cols], preferred_element_type=F32
        )
        layer = [(base + conds[e, :, cols]).astype(BF16) for e in range(EVALS)]
        fake = jnp.dot(layer[0], w_fake[cols, :], preferred_element_type=F32)
        teach = jnp.dot(jnp.concatenate(layer[1:], axis=0), w_teach[cols, :], preferred_element_type=F32)
        acc_fake = fake if c == 0 else acc_fake + fake
        acc_teach = teach if c == 0 else acc_teach + teach

    partial = [acc_fake, acc_teach[:tokens], acc_teach[tokens:]]
    for e in range(EVALS):
        q_part = partial[e][:, :head_dim].reshape(n_seq, n_mp, per_dev, head_dim)
        k_part = partial[e][:, head_dim : 2 * head_dim].astype(BF16)
        v_part = partial[e][:, 2 * head_dim :].astype(BF16)
        for slot in (e,) if e < EVALS - 1 else range(e, n_group):
            for k in range(n_mp):
                part_out[slot, k, :tokens] = k_part
                part_out[slot, k, tokens : 2 * tokens] = v_part
                part_out[slot, k, 2 * tokens :] = q_part[:, k].reshape(queries, head_dim).astype(BF16)
    part_copies = [
        push(
            part_out.at[at_group(dg), at_mp(dm)],
            part_in.at[g, m],
            part_send.at[dg, dm],
            part_recv.at[dg, dm],
            (at_group(dg), s, at_mp(dm)),
        )
        for dg in reversed(range(n_group))
        for dm in reversed(range(n_mp))
        if dg or dm
    ]
    part_in[g, m] = part_out[g, m]
    is_fake = g == 0
    out_t = jnp.where(is_fake, fake_out_ref[0], teacher_out_ref[0])
    coeff = jnp.where(
        is_fake, 1.0, jnp.where(g == 1, -guidance, jnp.where(g == 2, guidance - 1.0, 0.0))
    )
    for copy in part_copies:
        copy.wait_recv()
    total = part_in[:, 0].astype(F32)
    for k in range(1, n_mp):
        total = total + part_in[:, k].astype(F32)
    total = total.astype(BF16)
    keys = total[:, :tokens].reshape(n_group * tokens, head_dim)
    values = total[:, tokens : 2 * tokens].reshape(n_group * tokens, head_dim)
    asked = total[:, 2 * tokens :].reshape(n_group * queries, head_dim)
    scores = lax.dot_general(
        asked, keys, (((1,), (1,)), ((), ())), preferred_element_type=F32
    ) / jnp.sqrt(F32(head_dim))
    top = jnp.max(scores, axis=-1, keepdims=True)
    expo = jnp.exp(scores - top)
    probs = (expo / jnp.sum(expo, axis=-1, keepdims=True)).astype(BF16)
    heads = jnp.dot(probs, values, preferred_element_type=F32).astype(BF16)
    velocity = coeff * lax.dot_general(heads, out_t, (((1,), (1,)), ((), ())), preferred_element_type=F32)

    vel_out[...] = velocity.reshape(n_group, n_seq, per_dev, -1)
    vel_copies = [
        push(
            vel_out.at[at_group(dg), at_seq(ds)],
            vel_in.at[g, s],
            vel_send.at[dg, ds],
            vel_recv.at[dg, ds],
            (at_group(dg), at_seq(ds), m),
        )
        for ds in reversed(range(n_seq))
        for dg in range(n_group)
        if dg or ds
    ]
    vel_in[g, s] = vel_out[g, s]
    scaled = hidden * rms
    for copy in vel_copies:
        copy.wait_recv()
    gap = jnp.sum(vel_in[...].reshape(n_group * n_seq, per_dev, -1), axis=0)
    gap_ref[0] = gap
    grad_normed = jnp.dot(gap.astype(BF16), head_t_ref[...], preferred_element_type=F32)
    grad_gain = grad_normed * gain
    grad = rms * (grad_gain - scaled * jnp.mean(scaled * grad_gain, axis=-1, keepdims=True))
    grad_ref[0] = grad.astype(BF16)

    for copy in lat_copies + cond_copies + part_copies + vel_copies:
        copy.wait_send()
    for copies in row_copies:
        for copy in copies:
            copy.wait_send()


def fused(
    gen_hidden,
    gen_gain,
    head_weight,
    noise,
    timestep,
    stream,
    patch_weight,
    conditions,
    teacher_qkv,
    teacher_out,
    fake_qkv,
    fake_out,
):
    n_group = lax.axis_size("group")
    n_seq = lax.axis_size("seq")
    n_mp = lax.axis_size("mp")
    per_dev = gen_hidden.shape[1]
    lat = head_weight.shape[1]
    ds_loc = stream.shape[2]
    head_dim = teacher_qkv.shape[3]
    share = n_mp * per_dev
    tokens = n_seq * share
    queries = n_seq * per_dev
    width = 3 * head_dim
    n_chunk = ds_loc // 512
    packed = 2 * tokens + queries
    n_plane = n_seq * n_mp - 1
    vmem = pl.BlockSpec(memory_space=pltpu.VMEM)
    hbm = pl.BlockSpec(memory_space=pltpu.HBM)
    smem = pl.BlockSpec(memory_space=pltpu.SMEM)
    dma = pltpu.SemaphoreType.DMA
    return pl.pallas_call(
        functools.partial(kernel, (n_group, n_seq, n_mp, n_chunk)),
        out_shape=(
            jax.ShapeDtypeStruct((1, per_dev, lat), F32),
            jax.ShapeDtypeStruct(gen_hidden.shape, BF16),
        ),
        in_specs=[hbm] * 4 + [smem] + [hbm] * 7,
        out_specs=(vmem, vmem),
        scratch_shapes=[
            pltpu.VMEM(gen_hidden.shape, BF16),
            pltpu.VMEM((1, gen_hidden.shape[2]), F32),
            pltpu.VMEM(head_weight.shape[::-1], BF16),
            pltpu.VMEM(noise.shape, F32),
            pltpu.VMEM(patch_weight.shape, BF16),
            pltpu.VMEM((1, lat, head_dim), BF16),
            pltpu.VMEM((1, lat, head_dim), BF16),
            pltpu.VMEM((n_seq, n_mp, per_dev, lat), F32),
            pltpu.VMEM((n_seq, share, ds_loc), BF16),
            pltpu.VMEM((n_group, 1, ds_loc), F32),
            pltpu.VMEM((ds_loc, width), BF16),
            pltpu.VMEM((ds_loc, width), BF16),
            pltpu.VMEM((n_group, n_mp, packed, head_dim), BF16),
            pltpu.VMEM((n_group, n_mp, packed, head_dim), BF16),
            pltpu.VMEM((n_group, n_seq, per_dev, lat), F32),
            pltpu.VMEM((n_group, n_seq, per_dev, lat), F32),
            dma((7,)),
            dma((8,)),
            dma((n_plane,)),
            dma((n_plane,)),
            dma((n_group - 1,)),
            dma((n_group - 1,)),
            dma((n_chunk, n_seq - 1)),
            dma((n_chunk, n_seq - 1)),
            dma((n_group, n_mp)),
            dma((n_group, n_mp)),
            dma((n_group, n_seq)),
            dma((n_group, n_seq)),
        ],
        compiler_params=pltpu.CompilerParams(
            collective_id=0, has_side_effects=True, vmem_limit_bytes=20 * 1024 * 1024
        ),
    )(*(
        a if a.dtype == jnp.int32 else pltpu.with_memory_space_constraint(a, pltpu.HBM)
        for a in (
        gen_hidden,
        gen_gain.reshape(1, -1),
        head_weight.T,
        noise,
        timestep,
        stream,
        patch_weight,
        conditions,
        teacher_qkv[:, :, 0, :].transpose(1, 0, 2),
        teacher_out.transpose(0, 2, 1),
        fake_qkv[:, :, 0, :].transpose(1, 0, 2),
        fake_out.transpose(0, 2, 1),
        )
    ))


def local(
    gen_hidden,
    gen_gain,
    head_weight,
    noise,
    timestep,
    stream,
    patch_weight,
    conditions,
    teacher_qkv,
    teacher_out,
    fake_qkv,
    fake_out,
):
    n_group = lax.axis_size("group")
    n_seq = lax.axis_size("seq")
    n_mp = lax.axis_size("mp")
    group_id = lax.axis_index("group")
    tok_dev = stream.shape[1]
    ds_loc = stream.shape[2]
    head_dim = teacher_qkv.shape[3]
    per_dev = gen_hidden.shape[1]
    width = 3 * head_dim
    hidden = gen_hidden[0].astype(jnp.float32)
    rms = 1.0 / jnp.sqrt(jnp.mean(hidden * hidden, axis=-1, keepdims=True) + eps)
    normed = (hidden * rms * gen_gain[None, :]).astype(jnp.bfloat16)
    clean = jnp.dot(normed, head_weight, preferred_element_type=jnp.float32)
    sigma = timestep[0].astype(jnp.float32) / 1000.0
    noised = ((1.0 - sigma) * clean + sigma * noise[0]).astype(jnp.bfloat16)
    is_fake = group_id == 0
    qkv_weight = jnp.where(is_fake, fake_qkv, teacher_qkv).reshape(ds_loc, width)
    out_weight = jnp.where(is_fake, fake_out, teacher_out)[0]
    coeff = jnp.where(
        group_id == 0,
        1.0,
        jnp.where(group_id == 1, -guidance, jnp.where(group_id == 2, guidance - 1.0, 0.0)),
    )
    cond_row = conditions[0][None, None, :]
    block_lat = lax.all_gather(noised, ("group", "mp"), axis=0, tiled=True)
    embedded = jnp.dot(block_lat, patch_weight, preferred_element_type=jnp.float32)
    rows = (stream[0].astype(jnp.float32) + embedded + cond_row[0]).astype(jnp.bfloat16)[None]
    queries_count = n_group * n_seq * per_dev
    piece = lax.all_gather(rows, "seq", axis=0, tiled=True)
    product = jnp.dot(piece.reshape(-1, ds_loc), qkv_weight, preferred_element_type=jnp.float32)
    partial_value = product.reshape(piece.shape[0], tok_dev, width)
    kv_part = partial_value[:, :, head_dim:].reshape(n_seq * tok_dev, 2 * head_dim)
    keys_vals = lax.psum(kv_part.astype(jnp.bfloat16), "mp")
    query_part = partial_value[:, :, :head_dim].reshape(n_seq, n_group, n_mp, per_dev, head_dim)
    query_part = query_part.transpose(2, 1, 0, 3, 4).reshape(n_mp * queries_count, head_dim)
    queries = lax.psum_scatter(
        query_part.astype(jnp.bfloat16), "mp", scatter_dimension=0, tiled=True
    )
    keys = keys_vals[:, :head_dim]
    values = keys_vals[:, head_dim:]
    scores = jnp.dot(queries, keys.T, preferred_element_type=jnp.float32) / jnp.sqrt(
        jnp.float32(head_dim)
    )
    top = jnp.max(scores, axis=-1, keepdims=True)
    expo = jnp.exp(scores - top)
    probs = (expo / jnp.sum(expo, axis=-1, keepdims=True)).astype(jnp.bfloat16)
    heads = jnp.dot(probs, values, preferred_element_type=jnp.float32).astype(jnp.bfloat16)
    weighted = coeff * jnp.dot(heads, out_weight, preferred_element_type=jnp.float32)
    score_gap = lax.psum_scatter(weighted, ("group", "seq"), scatter_dimension=0, tiled=True)
    gap_in = score_gap.astype(jnp.bfloat16)
    grad_normed = jnp.dot(gap_in, head_weight.T, preferred_element_type=jnp.float32)
    scaled = hidden * rms
    grad_gain = grad_normed * gen_gain[None, :]
    grad_hidden = rms * (grad_gain - scaled * jnp.mean(scaled * grad_gain, axis=-1, keepdims=True))
    return (score_gap[None], grad_hidden.astype(jnp.bfloat16)[None])


def solution(mesh):
    placed = (
        P("seq", ("group", "mp"), None),
        P(),
        P(),
        P("seq", ("group", "mp"), None),
        P(),
        P("seq", None, "mp"),
        P(None, "mp"),
        P("group", "mp"),
        P("mp", None, "seq", None),
        P("seq", None, None),
        P("mp", None, "seq", None),
        P("seq", None, None),
    )
    n_group, n_seq, n_mp = mesh.shape["group"], mesh.shape["seq"], mesh.shape["mp"]

    def part(*arrays):
        per_dev, ds_loc = arrays[0].shape[1], arrays[5].shape[2]
        tiled = per_dev % 8 == 0 and n_mp * per_dev % 16 == 0 and n_seq * per_dev % 16 == 0
        small = n_group > 1 and n_seq > 1 and n_mp > 1 and n_group >= EVALS
        if tiled and small and ds_loc % 512 == 0:
            return fused(*arrays)
        return local(*arrays)

    return jax.shard_map(
        part,
        mesh=mesh,
        in_specs=placed,
        out_specs=(P("seq", ("group", "mp"), None), P("seq", ("group", "mp"), None)),
        check_vma=False,
    )
```

```python
import functools

import jax
import jax.numpy as jnp
from jax import lax
from jax.experimental import pallas as pl
from jax.experimental.pallas import tpu as pltpu
from jax.sharding import PartitionSpec as P

guidance = 3.0
eps = 1e-06
MESH = pl.DeviceIdType.MESH
F32 = jnp.float32
BF16 = jnp.bfloat16
EVALS = 3


def run_if(needed, action):
    @pl.when(needed)
    def _():
        action()


def kernel(
    sizes,
    hid_hbm,
    gain_hbm,
    head_t_hbm,
    noise_hbm,
    time_ref,
    stream_ref,
    patch_hbm,
    cond_ref,
    teacher_ref,
    teacher_out_hbm,
    fake_ref,
    fake_out_hbm,
    gap_ref,
    grad_ref,
    hid_ref,
    gain_ref,
    head_t_ref,
    noise_ref,
    patch_ref,
    teacher_out_ref,
    fake_out_ref,
    latents,
    rows,
    conds,
    w_fake,
    w_teach,
    part_out,
    part_in,
    vel_out,
    vel_in,
    small_sem,
    local_sem,
    lat_send,
    lat_recv,
    cond_send,
    cond_recv,
    row_send,
    row_recv,
    hand_send,
    part_send,
    part_recv,
    vel_send,
    vel_recv,
):
    n_group, n_seq, n_mp, n_chunk = sizes
    g = lax.axis_index("group")
    s = lax.axis_index("seq")
    m = lax.axis_index("mp")
    per_dev = hid_ref.shape[1]
    ds_loc = stream_ref.shape[2]
    share = n_mp * per_dev
    tokens = n_seq * share
    queries = n_seq * per_dev
    head_dim = teacher_ref.shape[2]
    chunk = ds_loc // n_chunk

    def at_seq(d):
        return lax.rem(s + d, n_seq)

    def at_mp(d):
        return lax.rem(m + d, n_mp)

    def at_group(d):
        return lax.rem(g + d, n_group)

    plane = [(ds, dm) for ds in range(n_seq) for dm in range(n_mp) if ds or dm]

    def push(src, dst, send, recv, device, needed=None):
        copy = pltpu.make_async_remote_copy(
            src_ref=src, dst_ref=dst, send_sem=send, recv_sem=recv, device_id=device, device_id_type=MESH
        )
        if needed is None:
            copy.start()
        else:
            run_if(needed, copy.start)
        return copy

    barrier = pltpu.get_barrier_semaphore()
    for ds, dm in plane:
        pl.semaphore_signal(barrier, inc=1, device_id=(g, at_seq(ds), at_mp(dm)), device_id_type=MESH)
    cross = [(dg, ds, 0) for dg in range(1, n_group) for ds in range(n_seq)]
    cross += [(dg, 0, dm) for dg in range(1, n_group) for dm in range(1, n_mp)]
    for dg, ds, dm in cross:
        pl.semaphore_signal(
            barrier, inc=1, device_id=(at_group(dg), at_seq(ds), at_mp(dm)), device_id_type=MESH
        )

    my_rows = pl.ds(pl.multiple_of(g * share, share), share)
    small = [
        pltpu.make_async_copy(src, dst, small_sem.at[i])
        for i, (src, dst) in enumerate(
            (
                (hid_hbm, hid_ref),
                (gain_hbm, gain_ref),
                (head_t_hbm, head_t_ref),
                (noise_hbm, noise_ref),
                (patch_hbm, patch_ref),
                (teacher_out_hbm, teacher_out_ref),
                (fake_out_hbm, fake_out_ref),
            )
        )
    ]
    own = [
        pltpu.make_async_copy(stream_ref.at[0, my_rows, :], rows.at[s], local_sem.at[0]),
        pltpu.make_async_copy(cond_ref, conds.at[g], local_sem.at[1]),
    ]
    for j in range(3):
        cols = pl.ds(j * head_dim, head_dim)
        own.append(pltpu.make_async_copy(fake_ref.at[j], w_fake.at[:, cols], local_sem.at[2 + j]))
        own.append(pltpu.make_async_copy(teacher_ref.at[j], w_teach.at[:, cols], local_sem.at[5 + j]))
    for copy in small[:4] + own[:2] + small[4:] + own[2:]:
        copy.start()
    for copy in small[:4]:
        copy.wait()

    hidden = hid_ref[0].astype(F32)
    gain = gain_ref[...]
    rms = 1.0 / jnp.sqrt(jnp.mean(hidden * hidden, axis=-1, keepdims=True) + eps)
    normed = (hidden * rms * gain).astype(BF16)
    clean = lax.dot_general(normed, head_t_ref[...], (((1,), (1,)), ((), ())), preferred_element_type=F32)
    sigma = jnp.full(clean.shape, time_ref[0], jnp.int32).astype(F32) / 1000.0
    noised = ((1.0 - sigma) * clean + sigma * noise_ref[0]).astype(BF16)
    latents[s, m] = noised.astype(F32)

    pl.semaphore_wait(barrier, len(plane) + len(cross))

    lat_copies = []
    for i, (ds, dm) in enumerate(plane):
        lat_copies.append(
            push(latents.at[s, m], latents.at[s, m], lat_send.at[i], lat_recv.at[i], (g, at_seq(ds), at_mp(dm)))
        )
    direct = [jnp.abs(at_seq(d) - s) != n_seq - 1 for d in range(1, n_seq)]
    inner = jnp.logical_and(s > 0, s < n_seq - 1)
    onward = lax.rem(3 * s + 5, n_seq)
    onward_recv = lax.rem(2 * s + 2, n_seq)
    handed = []
    cond_copies = []
    row_copies = []
    for c in range(n_chunk):
        cols = pl.ds(c * chunk, chunk)
        group_of = []
        for d in range(1, n_seq):
            group_of.append(
                push(
                    stream_ref.at[0, my_rows, cols],
                    rows.at[s, :, cols],
                    row_send.at[c, d - 1],
                    row_recv.at[c, d - 1],
                    (g, at_seq(d), m),
                    direct[d - 1],
                )
            )
        row_copies.append(group_of)
        if c == 0:
            for d in range(1, n_group):
                cond_copies.append(
                    push(cond_ref, conds.at[g], cond_send.at[d - 1], cond_recv.at[d - 1], (at_group(d), s, m))
                )

    for copy in lat_copies:
        copy.wait_recv()
    lat_all = latents[...].reshape(tokens, -1).astype(BF16)
    for copy in own + small[4:]:
        copy.wait()
    for copy in cond_copies:
        copy.wait_recv()

    acc_fake = None
    acc_teach = None
    for c in range(n_chunk):
        cols = pl.ds(c * chunk, chunk)
        row_copies[c][1].wait_recv()
        handed.append(
            push(
                rows.at[at_seq(2), :, cols],
                rows.at[at_seq(2), :, cols],
                hand_send.at[c],
                row_recv.at[c, onward_recv],
                (g, onward, m),
                inner,
            )
        )
        row_copies[c][0].wait_recv()
        row_copies[c][2].wait_recv()
        base = rows[:, :, cols].reshape(tokens, chunk).astype(F32) + jnp.dot(
            lat_all, patch_ref[:, cols], preferred_element_type=F32
        )
        layer = [(base + conds[e, :, cols]).astype(BF16) for e in range(EVALS)]
        fake = jnp.dot(layer[0], w_fake[cols, :], preferred_element_type=F32)
        teach = jnp.dot(jnp.concatenate(layer[1:], axis=0), w_teach[cols, :], preferred_element_type=F32)
        acc_fake = fake if c == 0 else acc_fake + fake
        acc_teach = teach if c == 0 else acc_teach + teach

    partial = [acc_fake, acc_teach[:tokens], acc_teach[tokens:]]
    for e in range(EVALS):
        q_part = partial[e][:, :head_dim].reshape(n_seq, n_mp, per_dev, head_dim)
        k_part = partial[e][:, head_dim : 2 * head_dim].astype(BF16)
        v_part = partial[e][:, 2 * head_dim :].astype(BF16)
        for slot in (e,) if e < EVALS - 1 else range(e, n_group):
            for k in range(n_mp):
                part_out[slot, k, :tokens] = k_part
                part_out[slot, k, tokens : 2 * tokens] = v_part
                part_out[slot, k, 2 * tokens :] = q_part[:, k].reshape(queries, head_dim).astype(BF16)
    part_copies = [
        push(
            part_out.at[at_group(dg), at_mp(dm)],
            part_in.at[g, m],
            part_send.at[dg, dm],
            part_recv.at[dg, dm],
            (at_group(dg), s, at_mp(dm)),
        )
        for dg in reversed(range(n_group))
        for dm in reversed(range(n_mp))
        if dg or dm
    ]
    part_in[g, m] = part_out[g, m]
    is_fake = g == 0
    out_t = jnp.where(is_fake, fake_out_ref[0], teacher_out_ref[0])
    coeff = jnp.where(
        is_fake, 1.0, jnp.where(g == 1, -guidance, jnp.where(g == 2, guidance - 1.0, 0.0))
    )
    for copy in part_copies:
        copy.wait_recv()
    total = part_in[:, 0].astype(F32)
    for k in range(1, n_mp):
        total = total + part_in[:, k].astype(F32)
    total = total.astype(BF16)
    keys = total[:, :tokens].reshape(n_group * tokens, head_dim)
    values = total[:, tokens : 2 * tokens].reshape(n_group * tokens, head_dim)
    asked = total[:, 2 * tokens :].reshape(n_group * queries, head_dim)
    scores = lax.dot_general(
        asked, keys, (((1,), (1,)), ((), ())), preferred_element_type=F32
    ) / jnp.sqrt(F32(head_dim))
    top = jnp.max(scores, axis=-1, keepdims=True)
    expo = jnp.exp(scores - top)
    probs = (expo / jnp.sum(expo, axis=-1, keepdims=True)).astype(BF16)
    heads = jnp.dot(probs, values, preferred_element_type=F32).astype(BF16)
    velocity = coeff * lax.dot_general(heads, out_t, (((1,), (1,)), ((), ())), preferred_element_type=F32)

    vel_out[...] = velocity.reshape(n_group, n_seq, per_dev, -1)
    vel_copies = [
        push(
            vel_out.at[at_group(dg), at_seq(ds)],
            vel_in.at[g, s],
            vel_send.at[dg, ds],
            vel_recv.at[dg, ds],
            (at_group(dg), at_seq(ds), m),
        )
        for ds in reversed(range(n_seq))
        for dg in range(n_group)
        if dg or ds
    ]
    vel_in[g, s] = vel_out[g, s]
    scaled = hidden * rms
    for copy in vel_copies:
        copy.wait_recv()
    gap = jnp.sum(vel_in[...].reshape(n_group * n_seq, per_dev, -1), axis=0)
    gap_ref[0] = gap
    grad_normed = jnp.dot(gap.astype(BF16), head_t_ref[...], preferred_element_type=F32)
    grad_gain = grad_normed * gain
    grad = rms * (grad_gain - scaled * jnp.mean(scaled * grad_gain, axis=-1, keepdims=True))
    grad_ref[0] = grad.astype(BF16)

    for copy in lat_copies + cond_copies + part_copies + vel_copies:
        copy.wait_send()
    for copies in row_copies:
        for needed, copy in zip(direct, copies):
            run_if(needed, copy.wait_send)
    for copy in handed:
        run_if(inner, copy.wait_send)


def fused(
    gen_hidden,
    gen_gain,
    head_weight,
    noise,
    timestep,
    stream,
    patch_weight,
    conditions,
    teacher_qkv,
    teacher_out,
    fake_qkv,
    fake_out,
):
    n_group = lax.axis_size("group")
    n_seq = lax.axis_size("seq")
    n_mp = lax.axis_size("mp")
    per_dev = gen_hidden.shape[1]
    lat = head_weight.shape[1]
    ds_loc = stream.shape[2]
    head_dim = teacher_qkv.shape[3]
    share = n_mp * per_dev
    tokens = n_seq * share
    queries = n_seq * per_dev
    width = 3 * head_dim
    n_chunk = ds_loc // 512
    packed = 2 * tokens + queries
    n_plane = n_seq * n_mp - 1
    vmem = pl.BlockSpec(memory_space=pltpu.VMEM)
    hbm = pl.BlockSpec(memory_space=pltpu.HBM)
    smem = pl.BlockSpec(memory_space=pltpu.SMEM)
    dma = pltpu.SemaphoreType.DMA
    return pl.pallas_call(
        functools.partial(kernel, (n_group, n_seq, n_mp, n_chunk)),
        out_shape=(
            jax.ShapeDtypeStruct((1, per_dev, lat), F32),
            jax.ShapeDtypeStruct(gen_hidden.shape, BF16),
        ),
        in_specs=[hbm] * 4 + [smem] + [hbm] * 7,
        out_specs=(vmem, vmem),
        scratch_shapes=[
            pltpu.VMEM(gen_hidden.shape, BF16),
            pltpu.VMEM((1, gen_hidden.shape[2]), F32),
            pltpu.VMEM(head_weight.shape[::-1], BF16),
            pltpu.VMEM(noise.shape, F32),
            pltpu.VMEM(patch_weight.shape, BF16),
            pltpu.VMEM((1, lat, head_dim), BF16),
            pltpu.VMEM((1, lat, head_dim), BF16),
            pltpu.VMEM((n_seq, n_mp, per_dev, lat), F32),
            pltpu.VMEM((n_seq, share, ds_loc), BF16),
            pltpu.VMEM((n_group, 1, ds_loc), F32),
            pltpu.VMEM((ds_loc, width), BF16),
            pltpu.VMEM((ds_loc, width), BF16),
            pltpu.VMEM((n_group, n_mp, packed, head_dim), BF16),
            pltpu.VMEM((n_group, n_mp, packed, head_dim), BF16),
            pltpu.VMEM((n_group, n_seq, per_dev, lat), F32),
            pltpu.VMEM((n_group, n_seq, per_dev, lat), F32),
            dma((7,)),
            dma((8,)),
            dma((n_plane,)),
            dma((n_plane,)),
            dma((n_group - 1,)),
            dma((n_group - 1,)),
            dma((n_chunk, n_seq - 1)),
            dma((n_chunk, n_seq - 1)),
            dma((n_chunk,)),
            dma((n_group, n_mp)),
            dma((n_group, n_mp)),
            dma((n_group, n_seq)),
            dma((n_group, n_seq)),
        ],
        compiler_params=pltpu.CompilerParams(
            collective_id=0, has_side_effects=True, vmem_limit_bytes=20 * 1024 * 1024
        ),
    )(*(
        a if a.dtype == jnp.int32 else pltpu.with_memory_space_constraint(a, pltpu.HBM)
        for a in (
        gen_hidden,
        gen_gain.reshape(1, -1),
        head_weight.T,
        noise,
        timestep,
        stream,
        patch_weight,
        conditions,
        teacher_qkv[:, :, 0, :].transpose(1, 0, 2),
        teacher_out.transpose(0, 2, 1),
        fake_qkv[:, :, 0, :].transpose(1, 0, 2),
        fake_out.transpose(0, 2, 1),
        )
    ))


def local(
    gen_hidden,
    gen_gain,
    head_weight,
    noise,
    timestep,
    stream,
    patch_weight,
    conditions,
    teacher_qkv,
    teacher_out,
    fake_qkv,
    fake_out,
):
    n_group = lax.axis_size("group")
    n_seq = lax.axis_size("seq")
    n_mp = lax.axis_size("mp")
    group_id = lax.axis_index("group")
    tok_dev = stream.shape[1]
    ds_loc = stream.shape[2]
    head_dim = teacher_qkv.shape[3]
    per_dev = gen_hidden.shape[1]
    width = 3 * head_dim
    hidden = gen_hidden[0].astype(jnp.float32)
    rms = 1.0 / jnp.sqrt(jnp.mean(hidden * hidden, axis=-1, keepdims=True) + eps)
    normed = (hidden * rms * gen_gain[None, :]).astype(jnp.bfloat16)
    clean = jnp.dot(normed, head_weight, preferred_element_type=jnp.float32)
    sigma = timestep[0].astype(jnp.float32) / 1000.0
    noised = ((1.0 - sigma) * clean + sigma * noise[0]).astype(jnp.bfloat16)
    is_fake = group_id == 0
    qkv_weight = jnp.where(is_fake, fake_qkv, teacher_qkv).reshape(ds_loc, width)
    out_weight = jnp.where(is_fake, fake_out, teacher_out)[0]
    coeff = jnp.where(
        group_id == 0,
        1.0,
        jnp.where(group_id == 1, -guidance, jnp.where(group_id == 2, guidance - 1.0, 0.0)),
    )
    cond_row = conditions[0][None, None, :]
    block_lat = lax.all_gather(noised, ("group", "mp"), axis=0, tiled=True)
    embedded = jnp.dot(block_lat, patch_weight, preferred_element_type=jnp.float32)
    rows = (stream[0].astype(jnp.float32) + embedded + cond_row[0]).astype(jnp.bfloat16)[None]
    queries_count = n_group * n_seq * per_dev
    piece = lax.all_gather(rows, "seq", axis=0, tiled=True)
    product = jnp.dot(piece.reshape(-1, ds_loc), qkv_weight, preferred_element_type=jnp.float32)
    partial_value = product.reshape(piece.shape[0], tok_dev, width)
    kv_part = partial_value[:, :, head_dim:].reshape(n_seq * tok_dev, 2 * head_dim)
    keys_vals = lax.psum(kv_part.astype(jnp.bfloat16), "mp")
    query_part = partial_value[:, :, :head_dim].reshape(n_seq, n_group, n_mp, per_dev, head_dim)
    query_part = query_part.transpose(2, 1, 0, 3, 4).reshape(n_mp * queries_count, head_dim)
    queries = lax.psum_scatter(
        query_part.astype(jnp.bfloat16), "mp", scatter_dimension=0, tiled=True
    )
    keys = keys_vals[:, :head_dim]
    values = keys_vals[:, head_dim:]
    scores = jnp.dot(queries, keys.T, preferred_element_type=jnp.float32) / jnp.sqrt(
        jnp.float32(head_dim)
    )
    top = jnp.max(scores, axis=-1, keepdims=True)
    expo = jnp.exp(scores - top)
    probs = (expo / jnp.sum(expo, axis=-1, keepdims=True)).astype(jnp.bfloat16)
    heads = jnp.dot(probs, values, preferred_element_type=jnp.float32).astype(jnp.bfloat16)
    weighted = coeff * jnp.dot(heads, out_weight, preferred_element_type=jnp.float32)
    score_gap = lax.psum_scatter(weighted, ("group", "seq"), scatter_dimension=0, tiled=True)
    gap_in = score_gap.astype(jnp.bfloat16)
    grad_normed = jnp.dot(gap_in, head_weight.T, preferred_element_type=jnp.float32)
    scaled = hidden * rms
    grad_gain = grad_normed * gen_gain[None, :]
    grad_hidden = rms * (grad_gain - scaled * jnp.mean(scaled * grad_gain, axis=-1, keepdims=True))
    return (score_gap[None], grad_hidden.astype(jnp.bfloat16)[None])


def solution(mesh):
    placed = (
        P("seq", ("group", "mp"), None),
        P(),
        P(),
        P("seq", ("group", "mp"), None),
        P(),
        P("seq", None, "mp"),
        P(None, "mp"),
        P("group", "mp"),
        P("mp", None, "seq", None),
        P("seq", None, None),
        P("mp", None, "seq", None),
        P("seq", None, None),
    )
    n_group, n_seq, n_mp = mesh.shape["group"], mesh.shape["seq"], mesh.shape["mp"]

    def part(*arrays):
        per_dev, ds_loc = arrays[0].shape[1], arrays[5].shape[2]
        tiled = per_dev % 8 == 0 and n_mp * per_dev % 16 == 0 and n_seq * per_dev % 16 == 0
        small = n_group > 1 and n_seq == 4 and n_mp > 1 and n_group >= EVALS
        if tiled and small and ds_loc % 512 == 0:
            return fused(*arrays)
        return local(*arrays)

    return jax.shard_map(
        part,
        mesh=mesh,
        in_specs=placed,
        out_specs=(P("seq", ("group", "mp"), None), P("seq", ("group", "mp"), None)),
        check_vma=False,
    )
```
